32 devices in a mesh: groups: 2 (over x), blk: 16 (over z, y, core).
Axes of the slice: x: 2, y: 2, z: 4, core: 2. Of those that a mesh axis runs over, the one named last changes fastest.
Arguments:
- records: bfloat16 [8192, 2048], P(('groups', 'blk')), parts along dimension 0, may hold values from -6 to 6
- dest: int32 [8192, 1], P(('groups', 'blk')), parts along dimension 0, may hold values from 0 to 15; in each aligned block of 256 rows (0 to 255, 256 to 511, ...) at most 32 rows name the same one
- slot: int32 [8192, 1], P(('groups', 'blk')), parts along dimension 0, may hold values from 0 to 255
- valid: int32 [8192, 1], P(('groups', 'blk')), parts along dimension 0, may hold values from 256 to 2048
- masks: int32 [2], replicated, may hold values from 1 to 15, as said below
Outputs:
- correlations: bfloat16 [2, 4096, 128, 128], P(None, ('groups', 'blk')), parts along dimension 1
The draws below stay inside these ranges and needn't reach their ends.
There are 2 independent parts, one for each index of `groups`. The reference program is written for one: setup_inputs(seed, part) draws one part's arguments, and reference() takes and returns one part's arrays. A program takes and returns all parts, laid end to end along the dimension named above; an argument that names none is the same for every part. Nothing has to cross between parts.
Inputs may be any that keep to these rules, and one draw needn't show every extreme that they name: `dest`: in the rows of one device no block is named more than 32 times. `masks`: 2 distinct numbers; one of them is 15.
All inputs are finite; a program needn't handle non-finite values.
Results may differ from the reference program's by a relative error of at most 0.0085.
Values may be sent and summed in bfloat16 or wider, within the bound.
A program may use at most 128 MiB of HBM per device.

```python
import math
import jax
import jax.numpy as jnp
import numpy as np
from jax import lax

CH = 128
NFFT = 2048
F = 256
LAGS = 128
W = 2
ROUNDS = 2
SEG_DEV = 256
CAP = 32
BLOCKS = 16
SEGMENTS = 4096
N_BLK = 16


def draw_masks(key, part):
    third = jax.random.fold_in(jax.random.fold_in(key, 11), 2)
    fourth = jax.random.fold_in(jax.random.fold_in(key, 11), 3)
    count = N_BLK - 1
    score = jax.random.randint(third, (count,), 0, 1 << 20, dtype=jnp.int32)
    score = score * N_BLK + jnp.arange(count, dtype=jnp.int32)
    score = score.at[count - 1].set(-1)
    picked = jnp.argsort(score, stable=True)[:ROUNDS].astype(jnp.int32) + 1
    order = jax.random.permutation(fourth, ROUNDS)
    return picked[order].astype(jnp.int32)


def touch_ends(drawn, key, smallest, top_value):
    longest = drawn.shape.index(max(drawn.shape))
    spots = []
    for shift in (0, 1):
        where = [jax.random.randint(jax.random.fold_in(key, axis), (), 0, length) for axis, length in enumerate(drawn.shape)]
        where[longest] = (where[longest] + shift) % drawn.shape[longest]
        spots.append(tuple(where))
    return drawn.at[spots[0]].set(smallest).at[spots[1]].set(top_value)


def levels(own_key, shape, cuts, low, largest):
    def one(axis_at, shards_of):
        heights = jax.random.uniform(jax.random.fold_in(jax.random.fold_in(own_key, 6), axis_at), (shards_of,), jnp.float32, low / len(cuts), largest / len(cuts))
        return jnp.repeat(jnp.exp(heights), shape[axis_at] // shards_of).reshape((-1,) + (1,) * (len(shape) - axis_at - 1))

    gain = one(*cuts[0])
    for cut in cuts[1:]:
        gain = gain * one(*cut)
    return gain


def assign_block(stream_key, own, number, rows, amount, top, reach, skew):
    sequence = jax.random.permutation(stream_key, amount)
    crowded, common = portions_of(amount, rows * top, reach, skew, True), portions_of(amount, rows * top, reach, skew, False)
    places = jnp.arange(amount)

    def named(lengths, offset_by):
        used = int((lengths > 0).sum())
        fixed = max(1, used // 4)
        passed = fixed + (places - fixed + offset_by * (used - fixed)) % max(1, amount - fixed)
        return jnp.zeros((amount,), jnp.int32).at[sequence[jnp.where(places < fixed, places, passed)]].set(jnp.asarray(lengths, jnp.int32))

    lengths = jnp.where(number % 4 == 0, named(crowded, number // 4), named(common, number - number // 4 - 1))
    mixed = jax.random.permutation(jax.random.fold_in(own, 3), amount)
    source_of, receiver = mixed[0:amount // 2 * 2:2], mixed[1:amount // 2 * 2:2]
    room = jnp.minimum(lengths[source_of] - 1, reach - lengths[receiver]) // 2
    room = jnp.where((source_of == sequence[0]) | (receiver == sequence[0]) | (lengths[receiver] == 0), 0, jnp.maximum(room, 0))
    passed = jax.random.randint(jax.random.fold_in(own, 4), (amount // 2,), 0, 1 << 20) % (room + 1)
    lengths = lengths.at[source_of].add(-passed).at[receiver].add(passed)
    items = jnp.searchsorted(jnp.cumsum(lengths), jnp.arange(rows * top), side="right").astype(jnp.int32)
    table = items.reshape(top, rows).T
    table = table[jax.random.permutation(jax.random.fold_in(own, 1), rows)]
    offset_by = jax.random.randint(jax.random.fold_in(own, 2), (rows, 1), 0, top)
    return jnp.take_along_axis(table, (jnp.arange(top)[None, :] + offset_by) % top, axis=1)


def portions_of(number_of, total, bound, skew, full):
    loads = [(1 << 20) // math.isqrt(grade ** skew) + 1 for grade in range(1, number_of + 1)]
    largest = bound if full else min(bound, max(-(-total // number_of), total * loads[0] // sum(loads)))
    least = 1 if total - largest >= number_of - 1 else 0
    holding, rest = [largest] + [least] * (number_of - 1), total - largest - least * (number_of - 1)
    while rest > 0:
        free = [i for i in range(1, number_of) if holding[i] < largest] or [i for i in range(1, number_of) if holding[i] < bound]
        mass, budget = sum([loads[i] for i in free]), rest
        for i in free:
            addition = min(bound - holding[i], max(1, budget * loads[i] // mass), rest)
            holding[i] = holding[i] + addition
            rest = rest - addition
    return np.array(holding)


def scatter_about(rng, shape, width, limit, cuts=(), kind=jnp.bfloat16):
    drawn = jax.random.normal(rng, shape, jnp.float32) * width
    if len(cuts) > 0:
        drawn = levels(rng, shape, cuts, -0.22, 0.18) * drawn
    return jnp.clip(drawn, min=-limit, max=limit).astype(kind)


def setup_inputs(seed: int = 0, part: int = 0) -> dict:
    arg_keys = jax.random.split(jax.random.key(seed), 6)
    part_keys = jax.random.split(jax.random.fold_in(arg_keys[5], part), 6)
    records = scatter_about(part_keys[0], (SEGMENTS, NFFT), 1.0, 6.0, ((0, 16),))
    dest_keys = jax.random.split(jax.random.fold_in(part_keys[1], 1), SEGMENTS // SEG_DEV)
    dest_turns = jax.random.permutation(jax.random.fold_in(part_keys[1], 3), SEGMENTS // SEG_DEV)
    dest = jax.vmap(lambda own, number: assign_block(jax.random.fold_in(part_keys[1], 2), own, number, SEG_DEV, BLOCKS, 1, CAP, 2))(dest_keys, dest_turns).reshape((SEGMENTS, 1))
    slot = touch_ends(jax.random.randint(part_keys[2], (SEGMENTS, 1), 0, CH * W), jax.random.fold_in(part_keys[2], 1), 0, (CH * W) - 1).astype(jnp.int32)
    valid = touch_ends(jax.random.randint(part_keys[3], (SEGMENTS, 1), NFFT // 8, NFFT + 1), jax.random.fold_in(part_keys[3], 1), NFFT // 8, NFFT).astype(jnp.int32)
    masks = draw_masks(jax.random.fold_in(arg_keys[5], 71), part)
    return dict(records=records, dest=dest, slot=slot, valid=valid, masks=masks)


def forward_table(nfft, bins):
    sample = jnp.arange(nfft, dtype=jnp.int32)[:, None]
    freq = jnp.arange(1, bins + 1, dtype=jnp.int32)[None, :]
    angle = (sample * freq % nfft).astype(jnp.float32) * (2.0 * math.pi / nfft)
    return jnp.concatenate([jnp.cos(angle), -jnp.sin(angle)], axis=1).astype(jnp.bfloat16)

def inverse_table(nfft, bins, lags):
    shift = (jnp.arange(lags, dtype=jnp.int32) - lags // 2) % nfft
    freq = jnp.arange(1, bins + 1, dtype=jnp.int32)[:, None]
    angle = (freq * shift[None, :] % nfft).astype(jnp.float32) * (2.0 * math.pi / nfft)
    return jnp.concatenate([jnp.cos(angle), -jnp.sin(angle)], axis=0).astype(jnp.bfloat16)

def correlate_pair(own, other, itable):
    bins = own.shape[2] // 2
    left = own.astype(jnp.float32)
    right = other.astype(jnp.float32)
    first = jnp.concatenate([left[..., :bins], left[..., bins:]], axis=1)
    second = jnp.concatenate([left[..., bins:], -left[..., :bins]], axis=1)
    both = jnp.concatenate([right[..., :bins], right[..., bins:]], axis=1)
    real_part = jnp.einsum('iwf,jwf->ijf', first, both)
    imag_part = jnp.einsum('iwf,jwf->ijf', second, both)
    cross = jnp.concatenate([real_part, imag_part], axis=-1).astype(jnp.bfloat16)
    chans = own.shape[0]
    scale = 1.0 / math.sqrt(own.shape[1] * bins)
    lagged = jnp.dot(cross.reshape(chans * chans, 2 * bins), itable, preferred_element_type=jnp.float32)
    return (lagged * scale).astype(jnp.bfloat16).reshape(chans, chans, -1)

def reference(records, dest, slot, valid, masks):
    window = jnp.arange(NFFT, dtype=jnp.int32)[None, :] < valid[:, 0:1]
    masked = records * window.astype(jnp.bfloat16)
    target = dest[:, 0] * (CH * W) + slot[:, 0]
    summed = jnp.zeros((BLOCKS * CH * W, NFFT), jnp.float32).at[target].add(masked.astype(jnp.float32))
    coverage = jnp.zeros((BLOCKS * CH * W, NFFT), jnp.float32).at[target].add(window.astype(jnp.float32))
    trace = summed / jnp.maximum(coverage, 1.0)
    meansq = lax.optimization_barrier(jnp.mean(trace * trace, axis=1, keepdims=True))
    normed = (trace * lax.rsqrt(meansq + 1e-06)).astype(jnp.bfloat16)
    spectrum = jnp.dot(normed, forward_table(NFFT, F), preferred_element_type=jnp.float32)
    real_part = spectrum[:, :F]
    imag_part = spectrum[:, F:]
    amplitude = lax.rsqrt(jnp.maximum(real_part * real_part + imag_part * imag_part, NFFT / 4.0))
    white = jnp.concatenate([real_part * amplitude, imag_part * amplitude], axis=1).astype(jnp.bfloat16)
    tiles = white.reshape(BLOCKS, CH, W, 2 * F)
    itable = inverse_table(NFFT, F, LAGS)
    results = []
    for step in range(ROUNDS):
        partner = jnp.arange(BLOCKS, dtype=jnp.int32) ^ masks[step]
        others = tiles[partner]
        out = lax.map(lambda pair: correlate_pair(pair[0], pair[1], itable), (tiles, others))
        results.append(out.reshape(BLOCKS * CH, CH, LAGS))
    return jnp.stack(results)
```

```python
import functools
import math

import jax
import jax.numpy as jnp
import numpy as np
from jax import lax
from jax.experimental import pallas as pl
from jax.experimental.pallas import tpu as pltpu
from jax.sharding import PartitionSpec as P

CH = 128
F = 256
LAGS = 128
W = 2
EXTRA = 128
VMEM = pl.BlockSpec(memory_space=pltpu.VMEM)


def forward_table(nfft, bins):
    sample = np.arange(nfft, dtype=np.int64)[:, None]
    freq = np.arange(1, bins + 1, dtype=np.int64)[None, :]
    angle = (sample * freq % nfft).astype(np.float32) * np.float32(2.0 * math.pi / nfft)
    return np.concatenate([np.cos(angle), -np.sin(angle)], axis=1).astype(jnp.bfloat16)


def lag_table(nfft, bins, lags):
    shift = (np.arange(lags, dtype=np.int64) - lags // 2) % nfft
    freq = np.arange(1, bins + 1, dtype=np.int64)[None, :]
    angle = (freq * shift[:, None] % nfft).astype(np.float32) * np.float32(2.0 * math.pi / nfft)
    return np.concatenate([np.cos(angle), -np.sin(angle)], axis=1).astype(jnp.bfloat16)


def pack_kernel(capacity, records_ref, dest_ref, slot_ref, valid_ref, out_ref):
    held, nfft = records_ref.shape
    dest, slot, valid = dest_ref[...], slot_ref[...], valid_ref[...]
    named = lax.broadcasted_iota(jnp.int32, (held, 128), 1) == dest
    onehot = named.astype(jnp.float32)
    before = lax.broadcasted_iota(jnp.int32, (held, held), 1) < lax.broadcasted_iota(
        jnp.int32, (held, held), 0
    )
    earlier = jnp.dot(
        before.astype(jnp.float32).astype(jnp.bfloat16),
        onehot.astype(jnp.bfloat16),
        preferred_element_type=jnp.float32,
    )
    rank = jnp.sum(earlier * onehot, axis=1, keepdims=True).astype(jnp.int32)
    position = dest * capacity + rank
    spots = out_ref.shape[0]
    place = lax.broadcasted_iota(jnp.int32, (held, spots), 1) == position
    place = place.astype(jnp.float32).T.astype(jnp.bfloat16)
    window = lax.broadcasted_iota(jnp.int32, (held, nfft), 1) < valid
    masked = jnp.where(window, records_ref[...].astype(jnp.float32), 0.0).astype(jnp.bfloat16)
    out_ref[:, :nfft] = jnp.dot(place, masked, preferred_element_type=jnp.float32).astype(
        jnp.bfloat16
    )
    lane = lax.broadcasted_iota(jnp.int32, (held, EXTRA), 1)
    labels = jnp.where(lane == 0, slot, jnp.where(lane == 1, valid >> 3, valid & 7))
    labels = labels.astype(jnp.float32).astype(jnp.bfloat16)
    out_ref[:, nfft:] = jnp.dot(place, labels, preferred_element_type=jnp.float32).astype(
        jnp.bfloat16
    )


def whiten_kernel(arrived_ref, table_ref, out_ref):
    spots = arrived_ref.shape[0]
    nfft = table_ref.shape[0]
    rows = CH * W
    labels = arrived_ref[:, nfft:].astype(jnp.float32)
    valid = (labels[:, 1:2] * 8.0 + labels[:, 2:3]).astype(jnp.int32)
    slot = labels.T[0:1, :].astype(jnp.int32)
    row = (slot & (W - 1)) * CH + slot // W
    select = lax.broadcasted_iota(jnp.int32, (rows, spots), 0) == row
    select = select.astype(jnp.float32).astype(jnp.bfloat16)
    summed = jnp.dot(select, arrived_ref[:, :nfft], preferred_element_type=jnp.float32)
    window = lax.broadcasted_iota(jnp.int32, (spots, nfft), 1) < valid
    window = window.astype(jnp.float32).astype(jnp.bfloat16)
    coverage = jnp.dot(select, window, preferred_element_type=jnp.float32)
    trace = summed / jnp.maximum(coverage, 1.0)
    meansq = jnp.mean(trace * trace, axis=1, keepdims=True)
    normed = (trace * lax.rsqrt(meansq + 1e-06)).astype(jnp.bfloat16)
    spectrum = jnp.dot(normed, table_ref[...], preferred_element_type=jnp.float32)
    real_part, imag_part = spectrum[:, :F], spectrum[:, F:]
    amplitude = lax.rsqrt(jnp.maximum(real_part * real_part + imag_part * imag_part, nfft / 4.0))
    real_part = (real_part * amplitude).astype(jnp.bfloat16)
    imag_part = (imag_part * amplitude).astype(jnp.bfloat16)
    for w in range(W):
        base = 2 * F * w
        out_ref[:, base : base + F] = real_part[w * CH : (w + 1) * CH]
        out_ref[:, base + F : base + 2 * F] = imag_part[w * CH : (w + 1) * CH]


def correlate_kernel(step, own_ref, other_ref, table_ref, out_ref, turned):
    scale = 1.0 / math.sqrt(W * F)
    cosine, sine = table_ref[:, :F], table_ref[:, F:]
    rounds = other_ref.shape[0] // CH

    def pair(index, carry):
        for half in range(2):
            mine = own_ref[0, pl.ds(index * 2 + half, 1), :].astype(jnp.bfloat16)
            rows = slice(half * LAGS, (half + 1) * LAGS)
            for w in range(W):
                base = 2 * F * w
                ur, ui = mine[:, base : base + F], mine[:, base + F : base + 2 * F]
                turned[rows, base : base + F] = cosine * ur + sine * ui
                turned[rows, base + F : base + 2 * F] = cosine * ui - sine * ur
        product = lax.dot_general(
            other_ref[...],
            turned[...],
            (((1,), (1,)), ((), ())),
            preferred_element_type=jnp.float32,
        )
        product = (product * scale).astype(jnp.bfloat16)
        for half in range(2):
            for r in range(rounds):
                out_ref[r, index * 2 + half] = product[
                    r * CH : (r + 1) * CH, half * LAGS : (half + 1) * LAGS
                ]
        return carry

    lax.fori_loop(0, step // 2, pair, 0)


def local(records, dest, slot, valid, masks):
    owners = lax.axis_size("blk")
    held, nfft = records.shape
    rounds = masks.shape[0]
    capacity = max(2, 2 * held // owners)
    spots = owners * capacity
    width = 2 * F * W
    big = pltpu.CompilerParams(vmem_limit_bytes=48 * 2**20)
    outgoing = pl.pallas_call(
        functools.partial(pack_kernel, capacity),
        out_shape=jax.ShapeDtypeStruct((spots, nfft + EXTRA), jnp.bfloat16),
        in_specs=[VMEM] * 4,
        out_specs=VMEM,
        compiler_params=big,
        name="pack",
    )(records, dest, slot, valid)
    arrived = lax.all_to_all(outgoing, "blk", split_axis=0, concat_axis=0, tiled=True)
    tile = pl.pallas_call(
        whiten_kernel,
        out_shape=jax.ShapeDtypeStruct((CH, width), jnp.bfloat16),
        in_specs=[VMEM] * 2,
        out_specs=VMEM,
        compiler_params=big,
        name="whiten",
    )(arrived, jnp.asarray(forward_table(nfft, F)))
    last = owners - 1
    top = 1 << (owners.bit_length() - 2)

    def swap(block, distance):
        return lax.ppermute(block, "blk", [(b, b ^ distance) for b in range(owners)])

    far = swap(tile, last)

    def branch(mask):
        if mask & top:
            return lambda mine, met: swap(met, last ^ mask)
        return lambda mine, met: swap(mine, mask)

    second = masks[0] ^ masks[1] ^ last
    near = lax.switch(second - 1, [branch(m) for m in range(1, last)], tile, far)
    first = masks[0] == last
    other = jnp.concatenate([jnp.where(first, far, near), jnp.where(first, near, far)], axis=0)
    step = 8
    return pl.pallas_call(
        functools.partial(correlate_kernel, step),
        grid=(CH // step,),
        out_shape=jax.ShapeDtypeStruct((rounds, CH, CH, LAGS), jnp.bfloat16),
        in_specs=[
            pl.BlockSpec((1, step, width), lambda i: (i, 0, 0)),
            pl.BlockSpec((rounds * CH, width), lambda i: (0, 0)),
            pl.BlockSpec((LAGS, 2 * F), lambda i: (0, 0)),
        ],
        out_specs=pl.BlockSpec((rounds, step, CH, LAGS), lambda i: (0, i, 0, 0)),
        scratch_shapes=[pltpu.VMEM((2 * LAGS, width), jnp.bfloat16)],
        compiler_params=big,
        name="correlate",
    )(
        tile.astype(jnp.float32).reshape(CH // step, step, width),
        other,
        jnp.asarray(lag_table(nfft, F, LAGS)),
    )


def solution(mesh):
    return jax.shard_map(
        local,
        mesh=mesh,
        in_specs=(
            P(("groups", "blk"), None),
            P(("groups", "blk"), None),
            P(("groups", "blk"), None),
            P(("groups", "blk"), None),
            P(),
        ),
        out_specs=P(None, ("groups", "blk"), None, None),
        check_vma=False,
    )
```

```python
import functools
import math

import jax
import jax.numpy as jnp
import numpy as np
from jax import lax
from jax.experimental import pallas as pl
from jax.experimental.pallas import tpu as pltpu
from jax.sharding import PartitionSpec as P

CH = 128
F = 256
LAGS = 128
W = 2
EXTRA = 128
VMEM = pl.BlockSpec(memory_space=pltpu.VMEM)


def forward_table(nfft, bins):
    sample = np.arange(nfft, dtype=np.int64)[:, None]
    freq = np.arange(1, bins + 1, dtype=np.int64)[None, :]
    angle = (sample * freq % nfft).astype(np.float32) * np.float32(2.0 * math.pi / nfft)
    return np.concatenate([np.cos(angle), -np.sin(angle)], axis=1).astype(jnp.bfloat16)


def lag_table(nfft, bins, lags):
    shift = (np.arange(lags, dtype=np.int64) - lags // 2) % nfft
    freq = np.arange(1, bins + 1, dtype=np.int64)[None, :]
    angle = (freq * shift[:, None] % nfft).astype(np.float32) * np.float32(2.0 * math.pi / nfft)
    return np.concatenate([np.cos(angle), -np.sin(angle)], axis=1).astype(jnp.bfloat16)


def pack_kernel(capacity, records_ref, dest_ref, slot_ref, valid_ref, out_ref):
    held, nfft = records_ref.shape
    dest, slot, valid = dest_ref[...], slot_ref[...], valid_ref[...]
    named = lax.broadcasted_iota(jnp.int32, (held, 128), 1) == dest
    onehot = named.astype(jnp.float32)
    before = lax.broadcasted_iota(jnp.int32, (held, held), 1) < lax.broadcasted_iota(
        jnp.int32, (held, held), 0
    )
    earlier = jnp.dot(
        before.astype(jnp.float32).astype(jnp.bfloat16),
        onehot.astype(jnp.bfloat16),
        preferred_element_type=jnp.float32,
    )
    rank = jnp.sum(earlier * onehot, axis=1, keepdims=True).astype(jnp.int32)
    position = dest * capacity + rank
    spots = out_ref.shape[0]
    place = lax.broadcasted_iota(jnp.int32, (held, spots), 1) == position
    place = place.astype(jnp.float32).T.astype(jnp.bfloat16)
    window = lax.broadcasted_iota(jnp.int32, (held, nfft), 1) < valid
    masked = jnp.where(window, records_ref[...].astype(jnp.float32), 0.0).astype(jnp.bfloat16)
    out_ref[:, :nfft] = jnp.dot(place, masked, preferred_element_type=jnp.float32).astype(
        jnp.bfloat16
    )
    lane = lax.broadcasted_iota(jnp.int32, (held, EXTRA), 1)
    labels = jnp.where(lane == 0, slot, jnp.where(lane == 1, valid >> 3, valid & 7))
    labels = labels.astype(jnp.float32).astype(jnp.bfloat16)
    out_ref[:, nfft:] = jnp.dot(place, labels, preferred_element_type=jnp.float32).astype(
        jnp.bfloat16
    )


def whiten_kernel(arrived_ref, table_ref, out_ref):
    spots = arrived_ref.shape[0]
    nfft = table_ref.shape[0]
    rows = CH * W
    labels = arrived_ref[:, nfft:].astype(jnp.float32)
    valid = (labels[:, 1:2] * 8.0 + labels[:, 2:3]).astype(jnp.int32)
    slot = labels.T[0:1, :].astype(jnp.int32)
    row = (slot & (W - 1)) * CH + slot // W
    select = lax.broadcasted_iota(jnp.int32, (rows, spots), 0) == row
    select = select.astype(jnp.float32).astype(jnp.bfloat16)
    summed = jnp.dot(select, arrived_ref[:, :nfft], preferred_element_type=jnp.float32)
    window = lax.broadcasted_iota(jnp.int32, (spots, nfft), 1) < valid
    window = window.astype(jnp.float32).astype(jnp.bfloat16)
    coverage = jnp.dot(select, window, preferred_element_type=jnp.float32)
    trace = summed / jnp.maximum(coverage, 1.0)
    meansq = jnp.mean(trace * trace, axis=1, keepdims=True)
    normed = (trace * lax.rsqrt(meansq + 1e-06)).astype(jnp.bfloat16)
    spectrum = jnp.dot(normed, table_ref[...], preferred_element_type=jnp.float32)
    real_part, imag_part = spectrum[:, :F], spectrum[:, F:]
    amplitude = lax.rsqrt(jnp.maximum(real_part * real_part + imag_part * imag_part, nfft / 4.0))
    real_part = (real_part * amplitude).astype(jnp.bfloat16)
    imag_part = (imag_part * amplitude).astype(jnp.bfloat16)
    for w in range(W):
        base = 2 * F * w
        out_ref[:, base : base + F] = real_part[w * CH : (w + 1) * CH]
        out_ref[:, base + F : base + 2 * F] = imag_part[w * CH : (w + 1) * CH]


def correlate_kernel(far_round_ref, own_ref, other_ref, table_ref, out_ref, turned):
    scale = 1.0 / math.sqrt(W * F)
    cosine, sine = table_ref[:, :F], table_ref[:, F:]
    far_round = far_round_ref[0]
    slots, step = turned.shape[0], own_ref.shape[1]

    for index in range(step // 2):
        at = index % slots
        for half in range(2):
            mine = own_ref[0, index * 2 + half : index * 2 + half + 1, :].astype(jnp.bfloat16)
            rows = slice(half * LAGS, (half + 1) * LAGS)
            for w in range(W):
                base = 2 * F * w
                ur, ui = mine[:, base : base + F], mine[:, base + F : base + 2 * F]
                turned[at, rows, base : base + F] = cosine * ur + sine * ui
                turned[at, rows, base + F : base + 2 * F] = cosine * ui - sine * ur
        product = lax.dot_general(
            other_ref[...],
            turned[at],
            (((1,), (1,)), ((), ())),
            preferred_element_type=jnp.float32,
        )
        product = (product * scale).astype(jnp.bfloat16)
        for half in range(2):
            lags = slice(half * LAGS, (half + 1) * LAGS)
            out_ref[far_round, index * 2 + half] = product[:CH, lags]
            out_ref[1 - far_round, index * 2 + half] = product[CH:, lags]


def local(records, dest, slot, valid, masks):
    owners = lax.axis_size("blk")
    held, nfft = records.shape
    rounds = masks.shape[0]
    capacity = max(2, 2 * held // owners)
    spots = owners * capacity
    width = 2 * F * W
    big = pltpu.CompilerParams(vmem_limit_bytes=48 * 2**20)
    outgoing = pl.pallas_call(
        functools.partial(pack_kernel, capacity),
        out_shape=jax.ShapeDtypeStruct((spots, nfft + EXTRA), jnp.bfloat16),
        in_specs=[VMEM] * 4,
        out_specs=VMEM,
        compiler_params=big,
        name="pack",
    )(records, dest, slot, valid)
    arrived = lax.all_to_all(outgoing, "blk", split_axis=0, concat_axis=0, tiled=True)
    tile = pl.pallas_call(
        whiten_kernel,
        out_shape=jax.ShapeDtypeStruct((CH, width), jnp.bfloat16),
        in_specs=[VMEM] * 2,
        out_specs=VMEM,
        compiler_params=big,
        name="whiten",
    )(arrived, jnp.asarray(forward_table(nfft, F)))
    last = owners - 1
    top = 1 << (owners.bit_length() - 2)

    def swap(block, distance):
        return lax.ppermute(block, "blk", [(b, b ^ distance) for b in range(owners)])

    far = swap(tile, last)

    def branch(mask):
        if mask & top:
            return lambda mine, met: swap(met, last ^ mask)
        return lambda mine, met: swap(mine, mask)

    second = masks[0] ^ masks[1] ^ last
    near = lax.switch(second - 1, [branch(m) for m in range(1, last)], tile, far)
    far_round = jnp.where(masks[0] == last, 0, 1).astype(jnp.int32).reshape(1)
    other = jnp.concatenate([far, near], axis=0)
    step = 16
    return pl.pallas_call(
        correlate_kernel,
        grid=(CH // step,),
        out_shape=jax.ShapeDtypeStruct((rounds, CH, CH, LAGS), jnp.bfloat16),
        in_specs=[
            pl.BlockSpec(memory_space=pltpu.SMEM),
            pl.BlockSpec((1, step, width), lambda i: (i, 0, 0)),
            pl.BlockSpec((rounds * CH, width), lambda i: (0, 0)),
            pl.BlockSpec((LAGS, 2 * F), lambda i: (0, 0)),
        ],
        out_specs=pl.BlockSpec((rounds, step, CH, LAGS), lambda i: (0, i, 0, 0)),
        scratch_shapes=[pltpu.VMEM((4, 2 * LAGS, width), jnp.bfloat16)],
        compiler_params=big,
        name="correlate",
    )(
        far_round,
        tile.astype(jnp.float32).reshape(CH // step, step, width),
        other,
        jnp.asarray(lag_table(nfft, F, LAGS)),
    )


def solution(mesh):
    return jax.shard_map(
        local,
        mesh=mesh,
        in_specs=(
            P(("groups", "blk"), None),
            P(("groups", "blk"), None),
            P(("groups", "blk"), None),
            P(("groups", "blk"), None),
            P(),
        ),
        out_specs=P(None, ("groups", "blk"), None, None),
        check_vma=False,
    )
```

```python
import functools
import math

import jax
import jax.numpy as jnp
import numpy as np
from jax import lax
from jax.experimental import pallas as pl
from jax.experimental.pallas import tpu as pltpu
from jax.sharding import PartitionSpec as P

CH = 128
F = 256
LAGS = 128
W = 2
EXTRA = 128
VMEM = pl.BlockSpec(memory_space=pltpu.VMEM)


def forward_table(nfft, bins):
    sample = np.arange(nfft, dtype=np.int64)[:, None]
    freq = np.arange(1, bins + 1, dtype=np.int64)[None, :]
    angle = (sample * freq % nfft).astype(np.float32) * np.float32(2.0 * math.pi / nfft)
    return np.concatenate([np.cos(angle), -np.sin(angle)], axis=1).astype(jnp.bfloat16)


def lag_table(nfft, bins, lags):
    shift = (np.arange(lags, dtype=np.int64) - lags // 2) % nfft
    freq = np.arange(1, bins + 1, dtype=np.int64)[None, :]
    angle = (freq * shift[:, None] % nfft).astype(np.float32) * np.float32(2.0 * math.pi / nfft)
    return np.concatenate([np.cos(angle), -np.sin(angle)], axis=1).astype(jnp.bfloat16)


def deliver_kernel(
    records_ref, dest_ref, slot_ref, valid_ref, table_hbm,
    tile_ref, far_ref,
    outgoing, arrived, summed, coverage, table, send_sem, recv_sem, own_sem, table_sem, far_sems,
):
    owners, capacity, wide = outgoing.shape
    held, nfft = records_ref.shape
    me = lax.axis_index("blk")

    def met(distance):
        other = me
        for k in range(owners.bit_length() - 1):
            if distance >> k & 1:
                other = other + (1 << k) * (1 - 2 * lax.rem(lax.div(me, 1 << k), 2))
        return other

    barrier = pltpu.get_barrier_semaphore()
    for distance in range(1, owners):
        pl.semaphore_signal(
            barrier, inc=1, device_id={"blk": met(distance)}, device_id_type=pl.DeviceIdType.MESH
        )
    fetch = pltpu.make_async_copy(table_hbm, table, table_sem)
    fetch.start()

    dest, slot, valid = dest_ref[...], slot_ref[...], valid_ref[...]
    onehot = (lax.broadcasted_iota(jnp.int32, (128, held), 0) == dest).astype(jnp.float32)
    before = lax.broadcasted_iota(jnp.int32, (held, held), 0) < lax.broadcasted_iota(
        jnp.int32, (held, held), 1
    )
    earlier = jnp.dot(
        onehot.astype(jnp.bfloat16),
        before.astype(jnp.float32).astype(jnp.bfloat16),
        preferred_element_type=jnp.float32,
    )
    rank = jnp.sum(earlier * onehot, axis=0, keepdims=True).astype(jnp.int32)
    position = dest * capacity + rank
    spots = owners * capacity
    place = lax.broadcasted_iota(jnp.int32, (spots, held), 0) == position
    place = place.astype(jnp.float32).astype(jnp.bfloat16)
    line = lax.broadcasted_iota(jnp.int32, (EXTRA, held), 0)
    labels = jnp.where(line == 0, slot, jnp.where(line == 1, valid >> 3, valid & 7))
    labels = labels.astype(jnp.float32).T.astype(jnp.bfloat16)
    packed = jnp.dot(place, records_ref[...], preferred_element_type=jnp.float32)
    outgoing[:, :, :nfft] = packed.astype(jnp.bfloat16).reshape(owners, capacity, nfft)
    packed = jnp.dot(place, labels, preferred_element_type=jnp.float32)
    outgoing[:, :, nfft:] = packed.astype(jnp.bfloat16).reshape(owners, capacity, EXTRA)

    pl.semaphore_wait(barrier, owners - 1)
    copies = {}
    for distance in range(owners - 1, 0, -1):
        copies[distance] = pltpu.make_async_remote_copy(
            src_ref=outgoing.at[met(distance)],
            dst_ref=arrived.at[me],
            send_sem=send_sem.at[distance],
            recv_sem=recv_sem.at[distance],
            device_id={"blk": met(distance)},
            device_id_type=pl.DeviceIdType.MESH,
        )
        copies[distance].start()
    own = pltpu.make_async_copy(outgoing.at[me], arrived.at[me], own_sem)
    own.start()

    half = owners // 2
    rows = CH * W

    def stack(base):
        block = arrived[pl.ds(base, half)].reshape(half * capacity, wide)
        marks = block[:, nfft:].astype(jnp.float32)
        reach = (marks[:, 1:2] * 8.0 + marks[:, 2:3]).astype(jnp.int32)
        goal = marks.T[0:1, :].astype(jnp.int32)
        goal = (goal & (W - 1)) * CH + lax.div(goal, W)
        select = lax.broadcasted_iota(jnp.int32, (rows, half * capacity), 0) == goal
        select = select.astype(jnp.float32).astype(jnp.bfloat16)
        window = lax.broadcasted_iota(jnp.int32, (half * capacity, nfft), 1) < reach
        window = window.astype(jnp.float32).astype(jnp.bfloat16)
        data = block[:, :nfft] * window
        return (
            jnp.dot(select, data, preferred_element_type=jnp.float32),
            jnp.dot(select, window, preferred_element_type=jnp.float32),
        )

    near_base = lax.div(me, half) * half
    own.wait()
    for distance in range(half - 1, 0, -1):
        copies[distance].wait_recv()
    summed[...], coverage[...] = stack(near_base)
    for distance in range(owners - 1, half - 1, -1):
        copies[distance].wait_recv()
    total, count = stack(half - near_base)
    trace = (summed[...] + total) / jnp.maximum(coverage[...] + count, 1.0)
    meansq = jnp.mean(trace * trace, axis=1, keepdims=True)
    normed = (trace * lax.rsqrt(meansq + 1e-06)).astype(jnp.bfloat16)
    fetch.wait()
    spectrum = jnp.dot(normed, table[...], preferred_element_type=jnp.float32)
    real_part, imag_part = spectrum[:, :F], spectrum[:, F:]
    amplitude = lax.rsqrt(jnp.maximum(real_part * real_part + imag_part * imag_part, nfft / 4.0))
    real_part = (real_part * amplitude).astype(jnp.bfloat16)
    imag_part = (imag_part * amplitude).astype(jnp.bfloat16)
    for w in range(W):
        base = 2 * F * w
        tile_ref[:, base : base + F] = real_part[w * CH : (w + 1) * CH]
        tile_ref[:, base + F : base + 2 * F] = imag_part[w * CH : (w + 1) * CH]
    across = pltpu.make_async_remote_copy(
        src_ref=tile_ref,
        dst_ref=far_ref,
        send_sem=far_sems.at[0],
        recv_sem=far_sems.at[1],
        device_id={"blk": met(owners - 1)},
        device_id_type=pl.DeviceIdType.MESH,
    )
    across.start()
    for distance in range(owners - 1, 0, -1):
        copies[distance].wait_send()
    across.wait()


def correlate_kernel(far_round_ref, own_ref, other_ref, table_ref, out_ref, turned):
    scale = 1.0 / math.sqrt(W * F)
    cosine, sine = table_ref[:, :F], table_ref[:, F:]
    far_round = far_round_ref[0]
    slots, step = turned.shape[0], own_ref.shape[1]

    for index in range(step // 2):
        at = index % slots
        for half in range(2):
            mine = own_ref[0, index * 2 + half : index * 2 + half + 1, :].astype(jnp.bfloat16)
            rows = slice(half * LAGS, (half + 1) * LAGS)
            for w in range(W):
                base = 2 * F * w
                ur, ui = mine[:, base : base + F], mine[:, base + F : base + 2 * F]
                turned[at, rows, base : base + F] = cosine * ur + sine * ui
                turned[at, rows, base + F : base + 2 * F] = cosine * ui - sine * ur
        product = lax.dot_general(
            other_ref[...],
            turned[at],
            (((1,), (1,)), ((), ())),
            preferred_element_type=jnp.float32,
        )
        product = (product * scale).astype(jnp.bfloat16)
        for half in range(2):
            lags = slice(half * LAGS, (half + 1) * LAGS)
            out_ref[far_round, index * 2 + half] = product[:CH, lags]
            out_ref[1 - far_round, index * 2 + half] = product[CH:, lags]


def local(records, dest, slot, valid, masks):
    owners = lax.axis_size("blk")
    held, nfft = records.shape
    rounds = masks.shape[0]
    capacity = max(16, 2 * held // owners)
    width = 2 * F * W
    big = pltpu.CompilerParams(vmem_limit_bytes=56 * 2**20)
    slots = pltpu.VMEM((owners, capacity, nfft + EXTRA), jnp.bfloat16)
    tile, far = pl.pallas_call(
        deliver_kernel,
        out_shape=[jax.ShapeDtypeStruct((CH, width), jnp.bfloat16)] * 2,
        in_specs=[VMEM] * 4 + [pl.BlockSpec(memory_space=pl.ANY)],
        out_specs=[VMEM] * 2,
        scratch_shapes=[
            slots,
            slots,
            pltpu.VMEM((CH * W, nfft), jnp.float32),
            pltpu.VMEM((CH * W, nfft), jnp.float32),
            pltpu.VMEM((nfft, 2 * F), jnp.bfloat16),
            pltpu.SemaphoreType.DMA((owners,)),
            pltpu.SemaphoreType.DMA((owners,)),
            pltpu.SemaphoreType.DMA,
            pltpu.SemaphoreType.DMA,
            pltpu.SemaphoreType.DMA((2,)),
        ],
        compiler_params=pltpu.CompilerParams(
            vmem_limit_bytes=56 * 2**20, collective_id=0, has_side_effects=True
        ),
        name="deliver",
    )(
        records,
        dest.reshape(1, held),
        slot.reshape(1, held),
        valid.reshape(1, held),
        jnp.asarray(forward_table(nfft, F)),
    )
    last = owners - 1
    top = 1 << (owners.bit_length() - 2)

    def swap(block, distance):
        return lax.ppermute(block, "blk", [(b, b ^ distance) for b in range(owners)])

    def branch(mask):
        if mask & top:
            return lambda mine, met: swap(met, last ^ mask)
        return lambda mine, met: swap(mine, mask)

    second = masks[0] ^ masks[1] ^ last
    near = lax.switch(second - 1, [branch(m) for m in range(1, last)], tile, far)
    far_round = jnp.where(masks[0] == last, 0, 1).astype(jnp.int32).reshape(1)
    other = jnp.concatenate([far, near], axis=0)
    step = 16
    return pl.pallas_call(
        correlate_kernel,
        grid=(CH // step,),
        out_shape=jax.ShapeDtypeStruct((rounds, CH, CH, LAGS), jnp.bfloat16),
        in_specs=[
            pl.BlockSpec(memory_space=pltpu.SMEM),
            pl.BlockSpec((1, step, width), lambda i: (i, 0, 0)),
            pl.BlockSpec((rounds * CH, width), lambda i: (0, 0)),
            pl.BlockSpec((LAGS, 2 * F), lambda i: (0, 0)),
        ],
        out_specs=pl.BlockSpec((rounds, step, CH, LAGS), lambda i: (0, i, 0, 0)),
        scratch_shapes=[pltpu.VMEM((4, 2 * LAGS, width), jnp.bfloat16)],
        compiler_params=big,
        name="correlate",
    )(
        far_round,
        tile.astype(jnp.float32).reshape(CH // step, step, width),
        other,
        jnp.asarray(lag_table(nfft, F, LAGS)),
    )


def solution(mesh):
    return jax.shard_map(
        local,
        mesh=mesh,
        in_specs=(
            P(("groups", "blk"), None),
            P(("groups", "blk"), None),
            P(("groups", "blk"), None),
            P(("groups", "blk"), None),
            P(),
        ),
        out_specs=P(None, ("groups", "blk"), None, None),
        check_vma=False,
    )
```
